32 devices in a mesh: expert: 4 (over y, x), dp: 8 (over z, core).
Axes of the slice: x: 2, y: 2, z: 4, core: 2. Of those that a mesh axis runs over, the one named last changes fastest.
Arguments:
- tokens: bfloat16 [512, 4096], P(('expert', 'dp')), may hold values from -6 to 6
- grad_out: bfloat16 [512, 4096], P(('expert', 'dp')), may hold values from -6 to 6
- gate_values: bfloat16 [512, 2], P(('expert', 'dp')), may hold values from 0.099609375 to 1
- routes: int32 [512, 2], P(('expert', 'dp')), may hold values from 0 to 7, all different within a row; in each aligned block of 16 rows (0 to 15, 16 to 31, ...) at most 8 rows name the same one
- gate_weight: bfloat16 [8, 1536, 4096], P('expert', 'dp'), may hold values from -0.09375 to 0.09375
- up_weight: bfloat16 [8, 1536, 4096], P('expert', 'dp'), may hold values from -0.09375 to 0.09375
- down_weight: bfloat16 [8, 1536, 4096], P('expert', 'dp'), may hold values from -0.15625 to 0.15625
Outputs:
- grad_tokens: bfloat16 [512, 4096], P(('expert', 'dp'))
- grad_gates: float32 [512, 2], P(('expert', 'dp'))
- grad_gate_weight: bfloat16 [8, 1536, 4096], P('expert', 'dp')
- grad_up_weight: bfloat16 [8, 1536, 4096], P('expert', 'dp')
- grad_down_weight: bfloat16 [8, 1536, 4096], P('expert', 'dp')
The draws below stay inside these ranges and needn't reach their ends.
Inputs may be any that keep to these rules, and one draw needn't show every extreme that they name: `routes`: each row names 2 different experts. In each aligned block of 16 rows (the rows of one device) no expert is named by more than 8 rows, a bound that some block reaches.
All inputs are finite; a program needn't handle non-finite values.
Results may differ from the reference program's by a relative error of at most 0.019.
Values may be sent and summed in bfloat16 or wider, within the bound.
A program may use at most 128 MiB of HBM per device.

```python
import math
import jax
import jax.numpy as jnp
import numpy as np
from jax import lax

D = 4096
H = 1536
KWIN = 2
TOK_DEV = 16
EXPERTS = 8
CAP = 8
SLICE = 192
TOKENS = 512
N_EXPERT = 4
N_DP = 8


def block_scale(rng, shape, cuts, low, largest):
    gain, own = 1.0, jax.random.fold_in(rng, 6)
    for axis_at, blocks in cuts:
        draws = jnp.exp(jax.random.uniform(jax.random.fold_in(own, axis_at), (blocks,), jnp.float32, low / len(cuts), largest / len(cuts)))
        gain = gain * jnp.repeat(draws, shape[axis_at] // blocks).reshape([-1 if axis == axis_at else 1 for axis in range(len(shape))])
    return gain


def shared_out(stream_key, own, number, rows, amount, top, bound, lean):
    ranking = jax.random.permutation(stream_key, amount)
    heavy_load, ordinary = portions_of(amount, rows * top, bound, lean, True), portions_of(amount, rows * top, bound, lean, False)
    places = jnp.arange(amount)

    def named(sizes, offset_by):
        used = int((sizes > 0).sum())
        fixed = max(1, used // 4)
        shifted = fixed + (places - fixed + offset_by * (used - fixed)) % max(1, amount - fixed)
        return jnp.zeros((amount,), jnp.int32).at[ranking[jnp.where(places < fixed, places, shifted)]].set(jnp.asarray(sizes, jnp.int32))

    sizes = jnp.where(number % 4 == 0, named(heavy_load, number // 4), named(ordinary, number - number // 4 - 1))
    mixed = jax.random.permutation(jax.random.fold_in(own, 3), amount)
    giver, taker = mixed[0:amount // 2 * 2:2], mixed[1:amount // 2 * 2:2]
    margin = jnp.minimum(sizes[giver] - 1, bound - sizes[taker]) // 2
    margin = jnp.where((giver == ranking[0]) | (taker == ranking[0]) | (sizes[taker] == 0), 0, jnp.maximum(margin, 0))
    shifted = jax.random.randint(jax.random.fold_in(own, 4), (amount // 2,), 0, 1 << 20) % (margin + 1)
    sizes = sizes.at[giver].add(-shifted).at[taker].add(shifted)
    labels = jnp.searchsorted(jnp.cumsum(sizes), jnp.arange(rows * top), side="right").astype(jnp.int32)
    listing = labels.reshape(top, rows).T
    listing = listing[jax.random.permutation(jax.random.fold_in(own, 1), rows)]
    offset_by = jax.random.randint(jax.random.fold_in(own, 2), (rows, 1), 0, top)
    return jnp.take_along_axis(listing, (jnp.arange(top)[None, :] + offset_by) % top, axis=1)


def portions_of(number_of, total, most, lean, full):
    weights = [(1 << 20) // math.isqrt(standing ** lean) + 1 for standing in range(1, number_of + 1)]
    largest = most if full else min(most, max(-(-total // number_of), total * weights[0] // sum(weights)))
    least = 1 if total - largest >= number_of - 1 else 0
    holding, spare = [largest] + [least] * (number_of - 1), total - largest - least * (number_of - 1)
    while spare > 0:
        movable = [i for i in range(1, number_of) if holding[i] < largest] or [i for i in range(1, number_of) if holding[i] < most]
        pool, left = sum([weights[i] for i in movable]), spare
        for i in movable:
            extra = min(most - holding[i], max(1, left * weights[i] // pool), spare)
            holding[i] = holding[i] + extra
            spare = spare - extra
    return np.array(holding)


def bell_draw(own_key, dims, deviation, most, shards=(), kind=jnp.bfloat16):
    drawn = deviation * jax.random.normal(own_key, dims, jnp.float32)
    if shards:
        drawn = drawn * block_scale(own_key, dims, shards, -0.22, 0.18)
    return jnp.clip(drawn, -most, most).astype(kind)


def setup_inputs(seed: int = 0) -> dict:
    splits = jax.random.split(jax.random.key(seed), 8)
    tokens = bell_draw(splits[0], (TOKENS, D), 1.0, 6.0, ((0, 32),))
    grad_out = bell_draw(splits[1], (TOKENS, D), 1.0, 6.0, ((0, 32),))
    gate_values = jnp.clip(jnp.exp(math.log(1.0) - 2.306499 * jax.random.uniform(splits[2], (TOKENS, KWIN), jnp.float32) ** block_scale(splits[2], (TOKENS, KWIN), ((0, 32),), -0.2, 0.2)), 0.099609375, 1.0).astype(jnp.bfloat16)
    routes_keys = jax.random.split(jax.random.fold_in(splits[3], 1), TOKENS // TOK_DEV)
    routes_turns = jax.random.permutation(jax.random.fold_in(splits[3], 3), TOKENS // TOK_DEV)
    routes = jax.vmap(lambda own, number: shared_out(jax.random.fold_in(splits[3], 2), own, number, TOK_DEV, EXPERTS, KWIN, CAP, 2))(routes_keys, routes_turns).reshape((TOKENS, KWIN))
    gate_weight = bell_draw(splits[4], (EXPERTS, H, D), D ** -0.5, 0.09375, ((0, 4), (1, 8)))
    up_weight = bell_draw(splits[5], (EXPERTS, H, D), D ** -0.5, 0.09375, ((0, 4), (1, 8)))
    down_weight = bell_draw(splits[6], (EXPERTS, H, D), H ** -0.5, 0.15625, ((0, 4), (1, 8)))
    return {"tokens": tokens, "grad_out": grad_out, "gate_values": gate_values, "routes": routes, "gate_weight": gate_weight, "up_weight": up_weight, "down_weight": down_weight}


def expert_terms(tokens, grad_out, flat_routes, flat_gates, gate_rows, up_rows, down_rows, expert):
    slot_total = N_EXPERT * N_DP * CAP
    picked = flat_routes == expert
    position = jnp.nonzero(picked, size=slot_total, fill_value=0)[0].astype(jnp.int32)
    live = (jnp.arange(slot_total) < jnp.sum(picked)).astype(jnp.float32)
    token_index = (position // KWIN).astype(jnp.int32)
    inputs = tokens[token_index]
    upstream = grad_out[token_index]
    weighting = (flat_gates[position] * live)[:, None]
    gate_pre = jnp.dot(inputs, gate_rows.T, preferred_element_type=jnp.float32)
    up_pre = jnp.dot(inputs, up_rows.T, preferred_element_type=jnp.float32)
    back_hidden = jnp.dot(upstream, down_rows.T, preferred_element_type=jnp.float32)
    sigmoid_gate = jax.nn.sigmoid(gate_pre)
    activated = gate_pre * sigmoid_gate
    hidden = activated * up_pre
    gate_grad = jnp.sum(back_hidden * hidden, axis=1)
    scaled = weighting * back_hidden
    grad_gate_pre = (scaled * up_pre * sigmoid_gate * (1.0 + gate_pre * (1.0 - sigmoid_gate))).astype(jnp.bfloat16)
    grad_up_pre = (scaled * activated).astype(jnp.bfloat16)
    weighted_hidden = (weighting * hidden).astype(jnp.bfloat16)
    split_gate = grad_gate_pre.astype(jnp.float32).reshape(slot_total, N_DP, SLICE)
    split_up = grad_up_pre.astype(jnp.float32).reshape(slot_total, N_DP, SLICE)
    gate_blocks = gate_rows.astype(jnp.float32).reshape(N_DP, SLICE, D)
    up_blocks = up_rows.astype(jnp.float32).reshape(N_DP, SLICE, D)
    pieces = jnp.einsum("rsh,shd->rsd", split_gate, gate_blocks, precision=lax.Precision.HIGHEST)
    pieces = pieces + jnp.einsum("rsh,shd->rsd", split_up, up_blocks, precision=lax.Precision.HIGHEST)
    pieces = lax.optimization_barrier(pieces.astype(jnp.bfloat16))
    row_grad = jnp.sum(pieces.astype(jnp.float32), axis=1).astype(jnp.bfloat16)
    grad_gate_rows = jnp.dot(grad_gate_pre.T, inputs, preferred_element_type=jnp.float32).astype(jnp.bfloat16)
    grad_up_rows = jnp.dot(grad_up_pre.T, inputs, preferred_element_type=jnp.float32).astype(jnp.bfloat16)
    grad_down_rows = jnp.dot(weighted_hidden.T, upstream, preferred_element_type=jnp.float32).astype(jnp.bfloat16)
    target = jnp.where(live > 0, position, TOKENS * KWIN).astype(jnp.int32)
    return row_grad, gate_grad, target, grad_gate_rows, grad_up_rows, grad_down_rows


def reference(tokens, grad_out, gate_values, routes, gate_weight, up_weight, down_weight):
    flat_routes = routes.reshape(-1)
    flat_gates = gate_values.reshape(-1).astype(jnp.float32)

    def per_expert(items):
        gate_rows, up_rows, down_rows, expert = items
        return expert_terms(tokens, grad_out, flat_routes, flat_gates, gate_rows, up_rows, down_rows, expert)

    experts_index = jnp.arange(EXPERTS, dtype=jnp.int32)
    row_grads, gate_grads, targets, grad_gate_weight, grad_up_weight, grad_down_weight = lax.map(
        per_expert, (gate_weight, up_weight, down_weight, experts_index))
    flat_targets = targets.reshape(-1)
    pair_grad = jnp.zeros((TOKENS * KWIN, D), jnp.float32).at[flat_targets].add(
        row_grads.reshape(-1, D).astype(jnp.float32), mode="drop")
    grad_tokens = jnp.sum(pair_grad.reshape(TOKENS, KWIN, D), axis=1).astype(jnp.bfloat16)
    grad_gates = jnp.zeros((TOKENS * KWIN,), jnp.float32).at[flat_targets].add(
        gate_grads.reshape(-1), mode="drop").reshape(TOKENS, KWIN)
    return grad_tokens, grad_gates, grad_gate_weight, grad_up_weight, grad_down_weight
```

```python
import jax
import jax.numpy as jnp
from jax import lax
from jax.sharding import PartitionSpec as P


def routed_rows(tokens, grad_out, gate_values, routes, gate_weight, up_weight, down_weight):
    tok_rows, model_width = tokens.shape
    chosen = routes.shape[1]
    local_experts = gate_weight.shape[0]
    groups = lax.axis_size("expert")
    replicas = lax.axis_size("dp")
    experts_all = local_experts * groups
    capacity = 2 * tok_rows * chosen // experts_all
    slot_count = experts_all * capacity
    flat_routes = routes.reshape(-1)
    same = flat_routes[:, None] == flat_routes[None, :]
    pair_index = jnp.arange(flat_routes.shape[0], dtype=jnp.int32)
    slot_rank = jnp.sum(
        (same & (pair_index[None, :] < pair_index[:, None])).astype(jnp.int32), axis=1
    )
    owner_col = flat_routes // local_experts
    local_id = flat_routes % local_experts
    slot_index = (local_id * groups + owner_col) * capacity + slot_rank
    placing = (jnp.arange(slot_count, dtype=jnp.int32)[:, None] == slot_index[None, :]).astype(
        jnp.float32
    )
    token_map = jnp.sum(placing.reshape(slot_count, tok_rows, chosen), axis=2).astype(jnp.bfloat16)
    slot_gates = jnp.dot(
        placing.astype(jnp.bfloat16), gate_values.reshape(-1), preferred_element_type=jnp.float32
    ).astype(jnp.bfloat16)
    x_slots = jnp.dot(token_map, tokens, preferred_element_type=jnp.float32).astype(jnp.bfloat16)
    dy_slots = jnp.dot(token_map, grad_out, preferred_element_type=jnp.float32).astype(jnp.bfloat16)
    block_shape = (local_experts, groups, capacity, model_width)
    arrived = (
        lax.all_to_all(
            x_slots.reshape(block_shape), "expert", split_axis=1, concat_axis=1, tiled=True
        ),
        lax.all_to_all(
            dy_slots.reshape(block_shape), "expert", split_axis=1, concat_axis=1, tiled=True
        ),
        lax.all_to_all(
            slot_gates.reshape(block_shape[:3]), "expert", split_axis=1, concat_axis=1, tiled=True
        ),
    )
    x_rows, dy_rows, gate_rows = (
        lax.all_gather(arrived[0], "dp", axis=2, tiled=True),
        lax.all_gather(arrived[1], "dp", axis=2, tiled=True),
        lax.all_gather(arrived[2], "dp", axis=2, tiled=True),
    )
    row_total = groups * replicas * capacity
    inputs = x_rows.reshape(local_experts, row_total, model_width)
    upstream = dy_rows.reshape(local_experts, row_total, model_width)
    weighting = gate_rows.reshape(local_experts, row_total).astype(jnp.float32)[..., None]
    gate_pre = jnp.einsum("lrd,lhd->lrh", inputs, gate_weight, preferred_element_type=jnp.float32)
    up_pre = jnp.einsum("lrd,lhd->lrh", inputs, up_weight, preferred_element_type=jnp.float32)
    back_hidden = jnp.einsum(
        "lrd,lhd->lrh", upstream, down_weight, preferred_element_type=jnp.float32
    )
    sigmoid_gate = jax.nn.sigmoid(gate_pre)
    activated = gate_pre * sigmoid_gate
    hidden = activated * up_pre
    gate_part = jnp.sum(back_hidden * hidden, axis=2)
    scaled = weighting * back_hidden
    grad_gate_pre = (
        scaled * up_pre * sigmoid_gate * (1.0 + gate_pre * (1.0 - sigmoid_gate))
    ).astype(jnp.bfloat16)
    grad_up_pre = (scaled * activated).astype(jnp.bfloat16)
    weighted_hidden = (weighting * hidden).astype(jnp.bfloat16)
    input_part = jnp.einsum(
        "lrh,lhd->lrd", grad_gate_pre, gate_weight, preferred_element_type=jnp.float32
    )
    input_part = input_part + jnp.einsum(
        "lrh,lhd->lrd", grad_up_pre, up_weight, preferred_element_type=jnp.float32
    )
    grad_gate_weight = jnp.einsum(
        "lrh,lrd->lhd", grad_gate_pre, inputs, preferred_element_type=jnp.float32
    ).astype(jnp.bfloat16)
    grad_up_weight = jnp.einsum(
        "lrh,lrd->lhd", grad_up_pre, inputs, preferred_element_type=jnp.float32
    ).astype(jnp.bfloat16)
    grad_down_weight = jnp.einsum(
        "lrh,lrd->lhd", weighted_hidden, upstream, preferred_element_type=jnp.float32
    ).astype(jnp.bfloat16)
    part_shape = (local_experts, groups, replicas * capacity, model_width)
    summed = lax.psum_scatter(
        input_part.reshape(part_shape).astype(jnp.bfloat16), "dp", scatter_dimension=2, tiled=True
    )
    returned = lax.all_to_all(summed, "expert", split_axis=1, concat_axis=1, tiled=True)
    returned = returned.reshape(slot_count, model_width)
    grad_tokens = lax.dot_general(
        token_map, returned, (((0,), (0,)), ((), ())), preferred_element_type=jnp.float32
    ).astype(jnp.bfloat16)
    gate_share = gate_part.reshape(local_experts, groups, replicas * capacity)
    gate_total = lax.psum(gate_share, "dp")
    own_gates = lax.dynamic_slice_in_dim(gate_total, lax.axis_index("dp") * capacity, capacity, 2)
    gate_back = lax.all_to_all(
        own_gates, "expert", split_axis=1, concat_axis=1, tiled=True
    ).reshape(slot_count)
    grad_gates = jnp.dot(gate_back, placing, precision=lax.Precision.HIGHEST).reshape(
        tok_rows, chosen
    )
    return (grad_tokens, grad_gates, grad_gate_weight, grad_up_weight, grad_down_weight)


def swap(values, masks):
    total = lax.axis_size("expert") * lax.axis_size("dp")
    pairs = [(i, i ^ masks[i % 2]) for i in range(total)]
    return lax.ppermute(values, ("expert", "dp"), pairs)


def swap_order():
    replicas, groups = lax.axis_size("dp"), lax.axis_size("expert")
    along_dp = []
    step = replicas // 2
    while step > 1:
        along_dp.append((step, step))
        step //= 2
    low, high = replicas, replicas * groups // 2
    across = [(low, high), (high, low)]
    return along_dp, across


def collect(own, axis):
    along_dp, across = swap_order()
    block = own
    for masks in along_dp:
        block = jnp.concatenate([block, swap(block, masks)], axis=axis)
    pieces = [block]
    for masks in across:
        pieces = pieces + [swap(piece, masks) for piece in pieces]
    half = jnp.concatenate(pieces, axis=axis)
    return half, swap(half, (1, 1))


def hand_out(half, other, axis):
    along_dp, across = swap_order()

    def plus(kept, came):
        return (kept.astype(jnp.float32) + came.astype(jnp.float32)).astype(kept.dtype)

    half = plus(half, swap(other, (1, 1)))
    for masks in across[::-1] + along_dp[::-1]:
        kept, sent = jnp.split(half, 2, axis=axis)
        half = plus(kept, swap(sent, masks))
    return half


def all_tokens(tokens, grad_out, gate_values, routes, gate_weight, up_weight, down_weight):
    model_width = tokens.shape[1]
    chosen = routes.shape[1]
    local_experts, part, _ = gate_weight.shape
    side = jnp.concatenate(
        [gate_values.astype(jnp.float32), routes.astype(jnp.float32)], axis=1
    ).T
    sides = collect(side, 1)
    xs = collect(tokens, 0)
    dys = collect(grad_out, 0)
    gate_mat = gate_weight.reshape(local_experts * part, model_width)
    up_mat = up_weight.reshape(local_experts * part, model_width)
    down_mat = down_weight.reshape(local_experts * part, model_width)
    over_width = (((1,), (1,)), ((), ()))
    over_rows = (((0,), (0,)), ((), ()))
    unit_expert = lax.broadcasted_iota(jnp.int32, (1, local_experts * part), 1) // part
    input_parts, gate_parts, lefts = [], [], []
    for x, dy, info in zip(xs, dys, sides):
        info = info.T
        gates = info[:, :chosen]
        named = info[:, chosen:].astype(jnp.int32) - lax.axis_index("expert") * local_experts
        gate_pre = lax.dot_general(x, gate_mat, over_width, preferred_element_type=jnp.float32)
        up_pre = lax.dot_general(x, up_mat, over_width, preferred_element_type=jnp.float32)
        back_hidden = lax.dot_general(
            dy, down_mat, over_width, preferred_element_type=jnp.float32
        )
        weighting = jnp.zeros(gate_pre.shape, jnp.float32)
        for k in range(chosen):
            weighting = weighting + jnp.where(
                named[:, k : k + 1] == unit_expert, gates[:, k : k + 1], 0.0
            )
        sigmoid_gate = jax.nn.sigmoid(gate_pre)
        activated = gate_pre * sigmoid_gate
        hidden = activated * up_pre
        product = back_hidden * hidden
        gate_parts.append(
            jnp.stack(
                [
                    jnp.sum(jnp.where(named[:, k : k + 1] == unit_expert, product, 0.0), axis=1)
                    for k in range(chosen)
                ],
                axis=0,
            )
        )
        scaled = weighting * back_hidden
        grad_gate_pre = (
            scaled * up_pre * sigmoid_gate * (1.0 + gate_pre * (1.0 - sigmoid_gate))
        ).astype(jnp.bfloat16)
        grad_up_pre = (scaled * activated).astype(jnp.bfloat16)
        weighted_hidden = (weighting * hidden).astype(jnp.bfloat16)
        input_part = jnp.dot(grad_gate_pre, gate_mat, preferred_element_type=jnp.float32)
        input_part = input_part + jnp.dot(grad_up_pre, up_mat, preferred_element_type=jnp.float32)
        input_parts.append(input_part.astype(jnp.bfloat16))
        lefts.append((grad_gate_pre, grad_up_pre, weighted_hidden))
    grad_tokens = hand_out(input_parts[0], input_parts[1], 0)
    grad_gates = hand_out(gate_parts[0], gate_parts[1], 1).T
    weight_grads = []
    for left, right in ((0, xs), (1, xs), (2, dys)):
        total = sum(
            lax.dot_general(lefts[i][left], right[i], over_rows, preferred_element_type=jnp.float32)
            for i in range(2)
        )
        weight_grads.append(total.astype(jnp.bfloat16).reshape(gate_weight.shape))
    return (grad_tokens, grad_gates, *weight_grads)


def per_device(tokens, grad_out, gate_values, routes, *weights):
    tok_rows, chosen = routes.shape
    capacity = 2 * tok_rows * chosen // (weights[0].shape[0] * lax.axis_size("expert"))
    slots = weights[0].shape[0] * capacity
    plan = all_tokens if tok_rows <= slots else routed_rows
    return plan(tokens, grad_out, gate_values, routes, *weights)


def solution(mesh):
    return jax.shard_map(
        per_device,
        mesh=mesh,
        in_specs=(
            P(("expert", "dp"), None),
            P(("expert", "dp"), None),
            P(("expert", "dp"), None),
            P(("expert", "dp"), None),
            P("expert", "dp", None),
            P("expert", "dp", None),
            P("expert", "dp", None),
        ),
        out_specs=(
            P(("expert", "dp"), None),
            P(("expert", "dp"), None),
            P("expert", "dp", None),
            P("expert", "dp", None),
            P("expert", "dp", None),
        ),
        check_vma=False,
    )
```

```python
import jax
import jax.numpy as jnp
from jax import lax
from jax.sharding import PartitionSpec as P


def routed_rows(tokens, grad_out, gate_values, routes, gate_weight, up_weight, down_weight):
    tok_rows, model_width = tokens.shape
    chosen = routes.shape[1]
    local_experts = gate_weight.shape[0]
    groups = lax.axis_size("expert")
    replicas = lax.axis_size("dp")
    experts_all = local_experts * groups
    capacity = 2 * tok_rows * chosen // experts_all
    slot_count = experts_all * capacity
    flat_routes = routes.reshape(-1)
    same = flat_routes[:, None] == flat_routes[None, :]
    pair_index = jnp.arange(flat_routes.shape[0], dtype=jnp.int32)
    slot_rank = jnp.sum(
        (same & (pair_index[None, :] < pair_index[:, None])).astype(jnp.int32), axis=1
    )
    owner_col = flat_routes // local_experts
    local_id = flat_routes % local_experts
    slot_index = (local_id * groups + owner_col) * capacity + slot_rank
    placing = (jnp.arange(slot_count, dtype=jnp.int32)[:, None] == slot_index[None, :]).astype(
        jnp.float32
    )
    token_map = jnp.sum(placing.reshape(slot_count, tok_rows, chosen), axis=2).astype(jnp.bfloat16)
    slot_gates = jnp.dot(
        placing.astype(jnp.bfloat16), gate_values.reshape(-1), preferred_element_type=jnp.float32
    ).astype(jnp.bfloat16)
    x_slots = jnp.dot(token_map, tokens, preferred_element_type=jnp.float32).astype(jnp.bfloat16)
    dy_slots = jnp.dot(token_map, grad_out, preferred_element_type=jnp.float32).astype(jnp.bfloat16)
    block_shape = (local_experts, groups, capacity, model_width)
    arrived = (
        lax.all_to_all(
            x_slots.reshape(block_shape), "expert", split_axis=1, concat_axis=1, tiled=True
        ),
        lax.all_to_all(
            dy_slots.reshape(block_shape), "expert", split_axis=1, concat_axis=1, tiled=True
        ),
        lax.all_to_all(
            slot_gates.reshape(block_shape[:3]), "expert", split_axis=1, concat_axis=1, tiled=True
        ),
    )
    x_rows, dy_rows, gate_rows = (
        lax.all_gather(arrived[0], "dp", axis=2, tiled=True),
        lax.all_gather(arrived[1], "dp", axis=2, tiled=True),
        lax.all_gather(arrived[2], "dp", axis=2, tiled=True),
    )
    row_total = groups * replicas * capacity
    inputs = x_rows.reshape(local_experts, row_total, model_width)
    upstream = dy_rows.reshape(local_experts, row_total, model_width)
    weighting = gate_rows.reshape(local_experts, row_total).astype(jnp.float32)[..., None]
    gate_pre = jnp.einsum("lrd,lhd->lrh", inputs, gate_weight, preferred_element_type=jnp.float32)
    up_pre = jnp.einsum("lrd,lhd->lrh", inputs, up_weight, preferred_element_type=jnp.float32)
    back_hidden = jnp.einsum(
        "lrd,lhd->lrh", upstream, down_weight, preferred_element_type=jnp.float32
    )
    sigmoid_gate = jax.nn.sigmoid(gate_pre)
    activated = gate_pre * sigmoid_gate
    hidden = activated * up_pre
    gate_part = jnp.sum(back_hidden * hidden, axis=2)
    scaled = weighting * back_hidden
    grad_gate_pre = (
        scaled * up_pre * sigmoid_gate * (1.0 + gate_pre * (1.0 - sigmoid_gate))
    ).astype(jnp.bfloat16)
    grad_up_pre = (scaled * activated).astype(jnp.bfloat16)
    weighted_hidden = (weighting * hidden).astype(jnp.bfloat16)
    input_part = jnp.einsum(
        "lrh,lhd->lrd", grad_gate_pre, gate_weight, preferred_element_type=jnp.float32
    )
    input_part = input_part + jnp.einsum(
        "lrh,lhd->lrd", grad_up_pre, up_weight, preferred_element_type=jnp.float32
    )
    grad_gate_weight = jnp.einsum(
        "lrh,lrd->lhd", grad_gate_pre, inputs, preferred_element_type=jnp.float32
    ).astype(jnp.bfloat16)
    grad_up_weight = jnp.einsum(
        "lrh,lrd->lhd", grad_up_pre, inputs, preferred_element_type=jnp.float32
    ).astype(jnp.bfloat16)
    grad_down_weight = jnp.einsum(
        "lrh,lrd->lhd", weighted_hidden, upstream, preferred_element_type=jnp.float32
    ).astype(jnp.bfloat16)
    part_shape = (local_experts, groups, replicas * capacity, model_width)
    summed = lax.psum_scatter(
        input_part.reshape(part_shape).astype(jnp.bfloat16), "dp", scatter_dimension=2, tiled=True
    )
    returned = lax.all_to_all(summed, "expert", split_axis=1, concat_axis=1, tiled=True)
    returned = returned.reshape(slot_count, model_width)
    grad_tokens = lax.dot_general(
        token_map, returned, (((0,), (0,)), ((), ())), preferred_element_type=jnp.float32
    ).astype(jnp.bfloat16)
    gate_share = gate_part.reshape(local_experts, groups, replicas * capacity)
    gate_total = lax.psum(gate_share, "dp")
    own_gates = lax.dynamic_slice_in_dim(gate_total, lax.axis_index("dp") * capacity, capacity, 2)
    gate_back = lax.all_to_all(
        own_gates, "expert", split_axis=1, concat_axis=1, tiled=True
    ).reshape(slot_count)
    grad_gates = jnp.dot(gate_back, placing, precision=lax.Precision.HIGHEST).reshape(
        tok_rows, chosen
    )
    return (grad_tokens, grad_gates, grad_gate_weight, grad_up_weight, grad_down_weight)


def swap(values, masks):
    total = lax.axis_size("expert") * lax.axis_size("dp")
    pairs = [(i, i ^ masks[i % 2]) for i in range(total)]
    return lax.ppermute(values, ("expert", "dp"), pairs)


def swap_order():
    replicas, groups = lax.axis_size("dp"), lax.axis_size("expert")
    along_dp = []
    step = replicas // 2
    while step > 1:
        along_dp.append((step, step))
        step //= 2
    low, high = replicas, replicas * groups // 2
    across = [(low, high), (high, low)]
    return along_dp, across


def collect(own, axis):
    along_dp, across = swap_order()
    block = own
    for masks in along_dp:
        block = jnp.concatenate([block, swap(block, masks)], axis=axis)
    pieces = [block]
    for masks in across:
        pieces = pieces + [swap(piece, masks) for piece in pieces]
    return pieces


def hand_out(half, other, axis):
    along_dp, across = swap_order()

    def plus(kept, came):
        return (kept.astype(jnp.float32) + came.astype(jnp.float32)).astype(kept.dtype)

    half = plus(half, swap(other, (1, 1)))
    for masks in across[::-1] + along_dp[::-1]:
        kept, sent = jnp.split(half, 2, axis=axis)
        half = plus(kept, swap(sent, masks))
    return half


def all_tokens(tokens, grad_out, gate_values, routes, gate_weight, up_weight, down_weight):
    model_width = tokens.shape[1]
    chosen = routes.shape[1]
    local_experts, part, _ = gate_weight.shape
    side = jnp.concatenate([gate_values, routes.astype(jnp.bfloat16)], axis=1)
    side = jnp.pad(side, ((0, 0), (0, 128 - 2 * chosen)))
    x_pieces = collect(jnp.concatenate([tokens, side], axis=1), 0)
    dy_pieces = collect(grad_out, 0)

    def both_cores(pieces):
        half = jnp.concatenate(pieces, axis=0)
        return half, swap(half, (1, 1))

    sides = both_cores([piece[:, model_width:] for piece in x_pieces])
    xs = both_cores([piece[:, :model_width] for piece in x_pieces])
    dys = both_cores(dy_pieces)
    gate_mat = gate_weight.reshape(local_experts * part, model_width)
    up_mat = up_weight.reshape(local_experts * part, model_width)
    down_mat = down_weight.reshape(local_experts * part, model_width)
    over_width = (((1,), (1,)), ((), ()))
    over_rows = (((0,), (0,)), ((), ()))
    unit_expert = lax.broadcasted_iota(jnp.int32, (1, local_experts * part), 1) // part
    input_parts, gate_parts, lefts = [], [], []
    for x, dy, info in zip(xs, dys, sides):
        gates = info[:, :chosen].astype(jnp.float32)
        named = info[:, chosen : 2 * chosen].astype(jnp.int32) - lax.axis_index("expert") * local_experts
        gate_pre = lax.dot_general(x, gate_mat, over_width, preferred_element_type=jnp.float32)
        up_pre = lax.dot_general(x, up_mat, over_width, preferred_element_type=jnp.float32)
        back_hidden = lax.dot_general(
            dy, down_mat, over_width, preferred_element_type=jnp.float32
        )
        weighting = jnp.zeros(gate_pre.shape, jnp.float32)
        for k in range(chosen):
            weighting = weighting + jnp.where(
                named[:, k : k + 1] == unit_expert, gates[:, k : k + 1], 0.0
            )
        sigmoid_gate = jax.nn.sigmoid(gate_pre)
        activated = gate_pre * sigmoid_gate
        hidden = activated * up_pre
        product = back_hidden * hidden
        gate_parts.append(
            jnp.stack(
                [
                    jnp.sum(jnp.where(named[:, k : k + 1] == unit_expert, product, 0.0), axis=1)
                    for k in range(chosen)
                ],
                axis=0,
            )
        )
        scaled = weighting * back_hidden
        grad_gate_pre = (
            scaled * up_pre * sigmoid_gate * (1.0 + gate_pre * (1.0 - sigmoid_gate))
        ).astype(jnp.bfloat16)
        grad_up_pre = (scaled * activated).astype(jnp.bfloat16)
        weighted_hidden = (weighting * hidden).astype(jnp.bfloat16)
        input_part = jnp.dot(grad_gate_pre, gate_mat, preferred_element_type=jnp.float32)
        input_part = input_part + jnp.dot(grad_up_pre, up_mat, preferred_element_type=jnp.float32)
        input_parts.append(input_part.astype(jnp.bfloat16))
        lefts.append((grad_gate_pre, grad_up_pre, weighted_hidden))
    grad_tokens = hand_out(input_parts[0], input_parts[1], 0)
    grad_gates = hand_out(gate_parts[0], gate_parts[1], 1).T
    weight_grads = []
    for left, right in ((0, xs), (1, xs), (2, dys)):
        total = sum(
            lax.dot_general(lefts[i][left], right[i], over_rows, preferred_element_type=jnp.float32)
            for i in range(2)
        )
        weight_grads.append(total.astype(jnp.bfloat16).reshape(gate_weight.shape))
    return (grad_tokens, grad_gates, *weight_grads)


def per_device(tokens, grad_out, gate_values, routes, *weights):
    tok_rows, chosen = routes.shape
    capacity = 2 * tok_rows * chosen // (weights[0].shape[0] * lax.axis_size("expert"))
    slots = weights[0].shape[0] * capacity
    plan = all_tokens if tok_rows <= slots else routed_rows
    return plan(tokens, grad_out, gate_values, routes, *weights)


def solution(mesh):
    return jax.shard_map(
        per_device,
        mesh=mesh,
        in_specs=(
            P(("expert", "dp"), None),
            P(("expert", "dp"), None),
            P(("expert", "dp"), None),
            P(("expert", "dp"), None),
            P("expert", "dp", None),
            P("expert", "dp", None),
            P("expert", "dp", None),
        ),
        out_specs=(
            P(("expert", "dp"), None),
            P(("expert", "dp"), None),
            P("expert", "dp", None),
            P("expert", "dp", None),
            P("expert", "dp", None),
        ),
        check_vma=False,
    )
```

```python
import jax
import jax.numpy as jnp
from jax import lax
from jax.sharding import PartitionSpec as P


def routed_rows(tokens, grad_out, gate_values, routes, gate_weight, up_weight, down_weight):
    tok_rows, model_width = tokens.shape
    chosen = routes.shape[1]
    local_experts = gate_weight.shape[0]
    groups = lax.axis_size("expert")
    replicas = lax.axis_size("dp")
    experts_all = local_experts * groups
    capacity = 2 * tok_rows * chosen // experts_all
    slot_count = experts_all * capacity
    flat_routes = routes.reshape(-1)
    same = flat_routes[:, None] == flat_routes[None, :]
    pair_index = jnp.arange(flat_routes.shape[0], dtype=jnp.int32)
    slot_rank = jnp.sum(
        (same & (pair_index[None, :] < pair_index[:, None])).astype(jnp.int32), axis=1
    )
    owner_col = flat_routes // local_experts
    local_id = flat_routes % local_experts
    slot_index = (local_id * groups + owner_col) * capacity + slot_rank
    placing = (jnp.arange(slot_count, dtype=jnp.int32)[:, None] == slot_index[None, :]).astype(
        jnp.float32
    )
    token_map = jnp.sum(placing.reshape(slot_count, tok_rows, chosen), axis=2).astype(jnp.bfloat16)
    slot_gates = jnp.dot(
        placing.astype(jnp.bfloat16), gate_values.reshape(-1), preferred_element_type=jnp.float32
    ).astype(jnp.bfloat16)
    x_slots = jnp.dot(token_map, tokens, preferred_element_type=jnp.float32).astype(jnp.bfloat16)
    dy_slots = jnp.dot(token_map, grad_out, preferred_element_type=jnp.float32).astype(jnp.bfloat16)
    block_shape = (local_experts, groups, capacity, model_width)
    arrived = (
        lax.all_to_all(
            x_slots.reshape(block_shape), "expert", split_axis=1, concat_axis=1, tiled=True
        ),
        lax.all_to_all(
            dy_slots.reshape(block_shape), "expert", split_axis=1, concat_axis=1, tiled=True
        ),
        lax.all_to_all(
            slot_gates.reshape(block_shape[:3]), "expert", split_axis=1, concat_axis=1, tiled=True
        ),
    )
    x_rows, dy_rows, gate_rows = (
        lax.all_gather(arrived[0], "dp", axis=2, tiled=True),
        lax.all_gather(arrived[1], "dp", axis=2, tiled=True),
        lax.all_gather(arrived[2], "dp", axis=2, tiled=True),
    )
    row_total = groups * replicas * capacity
    inputs = x_rows.reshape(local_experts, row_total, model_width)
    upstream = dy_rows.reshape(local_experts, row_total, model_width)
    weighting = gate_rows.reshape(local_experts, row_total).astype(jnp.float32)[..., None]
    gate_pre = jnp.einsum("lrd,lhd->lrh", inputs, gate_weight, preferred_element_type=jnp.float32)
    up_pre = jnp.einsum("lrd,lhd->lrh", inputs, up_weight, preferred_element_type=jnp.float32)
    back_hidden = jnp.einsum(
        "lrd,lhd->lrh", upstream, down_weight, preferred_element_type=jnp.float32
    )
    sigmoid_gate = jax.nn.sigmoid(gate_pre)
    activated = gate_pre * sigmoid_gate
    hidden = activated * up_pre
    gate_part = jnp.sum(back_hidden * hidden, axis=2)
    scaled = weighting * back_hidden
    grad_gate_pre = (
        scaled * up_pre * sigmoid_gate * (1.0 + gate_pre * (1.0 - sigmoid_gate))
    ).astype(jnp.bfloat16)
    grad_up_pre = (scaled * activated).astype(jnp.bfloat16)
    weighted_hidden = (weighting * hidden).astype(jnp.bfloat16)
    input_part = jnp.einsum(
        "lrh,lhd->lrd", grad_gate_pre, gate_weight, preferred_element_type=jnp.float32
    )
    input_part = input_part + jnp.einsum(
        "lrh,lhd->lrd", grad_up_pre, up_weight, preferred_element_type=jnp.float32
    )
    grad_gate_weight = jnp.einsum(
        "lrh,lrd->lhd", grad_gate_pre, inputs, preferred_element_type=jnp.float32
    ).astype(jnp.bfloat16)
    grad_up_weight = jnp.einsum(
        "lrh,lrd->lhd", grad_up_pre, inputs, preferred_element_type=jnp.float32
    ).astype(jnp.bfloat16)
    grad_down_weight = jnp.einsum(
        "lrh,lrd->lhd", weighted_hidden, upstream, preferred_element_type=jnp.float32
    ).astype(jnp.bfloat16)
    part_shape = (local_experts, groups, replicas * capacity, model_width)
    summed = lax.psum_scatter(
        input_part.reshape(part_shape).astype(jnp.bfloat16), "dp", scatter_dimension=2, tiled=True
    )
    returned = lax.all_to_all(summed, "expert", split_axis=1, concat_axis=1, tiled=True)
    returned = returned.reshape(slot_count, model_width)
    grad_tokens = lax.dot_general(
        token_map, returned, (((0,), (0,)), ((), ())), preferred_element_type=jnp.float32
    ).astype(jnp.bfloat16)
    gate_share = gate_part.reshape(local_experts, groups, replicas * capacity)
    gate_total = lax.psum(gate_share, "dp")
    own_gates = lax.dynamic_slice_in_dim(gate_total, lax.axis_index("dp") * capacity, capacity, 2)
    gate_back = lax.all_to_all(
        own_gates, "expert", split_axis=1, concat_axis=1, tiled=True
    ).reshape(slot_count)
    grad_gates = jnp.dot(gate_back, placing, precision=lax.Precision.HIGHEST).reshape(
        tok_rows, chosen
    )
    return (grad_tokens, grad_gates, grad_gate_weight, grad_up_weight, grad_down_weight)


def swap(values, masks):
    total = lax.axis_size("expert") * lax.axis_size("dp")
    pairs = [(i, i ^ masks[i % 2]) for i in range(total)]
    return lax.ppermute(values, ("expert", "dp"), pairs)


def swap_order():
    replicas, groups = lax.axis_size("dp"), lax.axis_size("expert")
    along_dp = []
    step = replicas // 2
    while step > 1:
        along_dp.append((step, step))
        step //= 2
    low, high = replicas, replicas * groups // 2
    across = [(low, high), (high, low)]
    return along_dp, across


def line_masks(along_dp):
    masks = [0]
    for step, _ in along_dp:
        masks = masks + [mask ^ step for mask in masks]
    return masks


def collect(own, axis):
    along_dp, across = swap_order()
    block = own
    for masks in along_dp:
        block = jnp.concatenate([block, swap(block, masks)], axis=axis)
    pieces = [block]
    for masks in across:
        pieces = pieces + [swap(piece, masks) for piece in pieces]
    return pieces


def hand_out(half, other, axis, direct):
    along_dp, across = swap_order()

    def plus(kept, came):
        return (kept.astype(jnp.float32) + came.astype(jnp.float32)).astype(kept.dtype)

    half = plus(half, swap(other, (1, 1)))
    for masks in across[::-1] + ([] if direct else along_dp[::-1]):
        kept, sent = jnp.split(half, 2, axis=axis)
        half = plus(kept, swap(sent, masks))
    if direct:
        masks = line_masks(along_dp)
        pieces = jnp.split(half, len(masks), axis=axis)
        total = sum(
            (swap(piece, (m, m)) if m else piece).astype(jnp.float32)
            for m, piece in zip(masks, pieces)
        )
        half = total.astype(half.dtype)
    return half


def all_tokens(tokens, grad_out, gate_values, routes, gate_weight, up_weight, down_weight):
    model_width = tokens.shape[1]
    chosen = routes.shape[1]
    local_experts, part, _ = gate_weight.shape
    side = jnp.concatenate([gate_values, routes.astype(jnp.bfloat16)], axis=1)
    side = jnp.pad(side, ((0, 0), (0, 128 - 2 * chosen)))
    x_pieces = collect(jnp.concatenate([tokens, side], axis=1), 0)
    dy_pieces = collect(grad_out, 0)

    def both_cores(pieces):
        half = jnp.concatenate(pieces, axis=0)
        return half, swap(half, (1, 1))

    sides = both_cores([piece[:, model_width:] for piece in x_pieces])
    xs = both_cores([piece[:, :model_width] for piece in x_pieces])
    dys = both_cores(dy_pieces)
    gate_mat = gate_weight.reshape(local_experts * part, model_width)
    up_mat = up_weight.reshape(local_experts * part, model_width)
    down_mat = down_weight.reshape(local_experts * part, model_width)
    over_width = (((1,), (1,)), ((), ()))
    over_rows = (((0,), (0,)), ((), ()))
    unit_expert = lax.broadcasted_iota(jnp.int32, (1, local_experts * part), 1) // part
    input_parts, gate_parts, lefts = [], [], []
    for x, dy, info in zip(xs, dys, sides):
        gates = info[:, :chosen].astype(jnp.float32)
        named = info[:, chosen : 2 * chosen].astype(jnp.int32) - lax.axis_index("expert") * local_experts
        gate_pre = lax.dot_general(x, gate_mat, over_width, preferred_element_type=jnp.float32)
        up_pre = lax.dot_general(x, up_mat, over_width, preferred_element_type=jnp.float32)
        back_hidden = lax.dot_general(
            dy, down_mat, over_width, preferred_element_type=jnp.float32
        )
        weighting = jnp.zeros(gate_pre.shape, jnp.float32)
        for k in range(chosen):
            weighting = weighting + jnp.where(
                named[:, k : k + 1] == unit_expert, gates[:, k : k + 1], 0.0
            )
        sigmoid_gate = jax.nn.sigmoid(gate_pre)
        activated = gate_pre * sigmoid_gate
        hidden = activated * up_pre
        product = back_hidden * hidden
        gate_parts.append(
            jnp.stack(
                [
                    jnp.sum(jnp.where(named[:, k : k + 1] == unit_expert, product, 0.0), axis=1)
                    for k in range(chosen)
                ],
                axis=0,
            )
        )
        scaled = weighting * back_hidden
        grad_gate_pre = (
            scaled * up_pre * sigmoid_gate * (1.0 + gate_pre * (1.0 - sigmoid_gate))
        ).astype(jnp.bfloat16)
        grad_up_pre = (scaled * activated).astype(jnp.bfloat16)
        weighted_hidden = (weighting * hidden).astype(jnp.bfloat16)
        input_part = jnp.dot(grad_gate_pre, gate_mat, preferred_element_type=jnp.float32)
        input_part = input_part + jnp.dot(grad_up_pre, up_mat, preferred_element_type=jnp.float32)
        input_parts.append(input_part.astype(jnp.bfloat16))
        lefts.append((grad_gate_pre, grad_up_pre, weighted_hidden))
    grad_tokens = hand_out(input_parts[0], input_parts[1], 0, True)
    grad_gates = hand_out(gate_parts[0], gate_parts[1], 1, False).T
    weight_grads = []
    for left, right in ((0, xs), (1, xs), (2, dys)):
        total = sum(
            lax.dot_general(lefts[i][left], right[i], over_rows, preferred_element_type=jnp.float32)
            for i in range(2)
        )
        weight_grads.append(total.astype(jnp.bfloat16).reshape(gate_weight.shape))
    return (grad_tokens, grad_gates, *weight_grads)


def per_device(tokens, grad_out, gate_values, routes, *weights):
    tok_rows, chosen = routes.shape
    capacity = 2 * tok_rows * chosen // (weights[0].shape[0] * lax.axis_size("expert"))
    slots = weights[0].shape[0] * capacity
    plan = all_tokens if tok_rows <= slots else routed_rows
    return plan(tokens, grad_out, gate_values, routes, *weights)


def solution(mesh):
    return jax.shard_map(
        per_device,
        mesh=mesh,
        in_specs=(
            P(("expert", "dp"), None),
            P(("expert", "dp"), None),
            P(("expert", "dp"), None),
            P(("expert", "dp"), None),
            P("expert", "dp", None),
            P("expert", "dp", None),
            P("expert", "dp", None),
        ),
        out_specs=(
            P(("expert", "dp"), None),
            P(("expert", "dp"), None),
            P("expert", "dp", None),
            P("expert", "dp", None),
            P("expert", "dp", None),
        ),
        check_vma=False,
    )
```
